32 devices in a mesh: seq: 8 (over z, x), tp: 4 (over y, core).
Axes of the slice: x: 2, y: 2, z: 4, core: 2. Of those that a mesh axis runs over, the one named last changes fastest.
Arguments:
- queries: bfloat16 [8192, 4096], P('seq', 'tp'), may hold values from -576 to 576
- group_cond: bfloat16 [128, 896], P('seq'), may hold values from -6 to 6
- nbr_shard: int32 [128, 2], P('seq'), may hold values from 0 to 7, all different within a row; in each aligned block of 16 rows (0 to 15, 16 to 31, ...) at most 4 rows name the same one
- nbr_row: int32 [128, 2], P('seq'), may hold values from 0 to 7
- database: bfloat16 [64, 16, 896], P('seq'), may hold values from -6 to 6
- enc_gain: bfloat16 [896], replicated, may hold values from 0.25 to 1.75
- w_in: bfloat16 [1792, 896], P('tp'), may hold values from -0.1875 to 0.1875
- w_out: bfloat16 [1792, 896], P('tp'), may hold values from -0.125 to 0.125
- w_kv: bfloat16 [2, 896, 4096], P(None, 'seq', 'tp'), may hold values from -0.1875 to 0.1875
Outputs:
- attended: bfloat16 [8192, 4096], P('seq', 'tp')
The draws below stay inside these ranges and needn't reach their ends.
Inputs may be any that keep to these rules, and one draw needn't show every extreme that they name: `nbr_shard`: in each aligned block of 16 rows no shard is named by more than 4 rows, and one shard reaches 4; each row names 2 different shards.
All inputs are finite; a program needn't handle non-finite values.
Results may differ from the reference program's by a relative error of at most 0.025.
Values may be sent and summed in bfloat16 or wider, within the bound.
A program may use at most 64 MiB of HBM per device.

```python
import math
import jax
import jax.numpy as jnp
import numpy as np
from jax import lax

E = 896
E_FF = 1792
HEADS_W = 32
HEAD = 128
GROUP = 64
K = 2
NL = 16
GRP_DEV = 16
CAP = 4
DB_DEV = 8
GROUPS = 128
TOKENS = 8192
DB_ROWS = 64
HQ = 4096
N_SEQ = 8


def draw_queries(key, part):
    key = jax.random.fold_in(key, 11)
    base_key = jax.random.fold_in(key, 0)
    values = jax.random.normal(base_key, (TOKENS, HQ), jnp.float32)
    values = jnp.clip(values, -6.0, 6.0)
    return values.astype(jnp.bfloat16)


def touch_ends(drawn, key, smallest, largest):
    extent = drawn.shape
    spot = [jax.random.randint(jax.random.fold_in(key, axis), (), 0, extent[axis]) for axis in range(len(extent))]
    drawn = drawn.at[tuple(spot)].set(smallest)
    longest = extent.index(max(extent))
    spot[longest] = (spot[longest] + 1) % extent[longest]
    return drawn.at[tuple(spot)].set(largest)


def block_scale(rng, dims, cuts, low, high):
    def one(axis_at, parts):
        draws = jax.random.uniform(jax.random.fold_in(jax.random.fold_in(rng, 6), axis_at), (parts,), jnp.float32, low / len(cuts), high / len(cuts))
        return jnp.repeat(jnp.exp(draws), dims[axis_at] // parts).reshape((-1,) + (1,) * (len(dims) - axis_at - 1))

    level = one(*cuts[0])
    for cut in cuts[1:]:
        level = level * one(*cut)
    return level


def assign_block(rng, own, number, rows, number_of, top, limit, skew):
    ranking = jax.random.permutation(rng, number_of)
    heavy_load, ordinary = portions_of(number_of, rows * top, limit, skew, True), portions_of(number_of, rows * top, limit, skew, False)
    places = jnp.arange(number_of)

    def named(tallies, offset_by):
        used = int((tallies > 0).sum())
        fixed = max(1, used // 4)
        shifted = fixed + (places - fixed + offset_by * (used - fixed)) % max(1, number_of - fixed)
        return jnp.zeros((number_of,), jnp.int32).at[ranking[jnp.where(places < fixed, places, shifted)]].set(jnp.asarray(tallies, jnp.int32))

    tallies = jnp.where(number % 4 == 0, named(heavy_load, number // 4), named(ordinary, number - number // 4 - 1))
    mixed = jax.random.permutation(jax.random.fold_in(own, 3), number_of)
    source_of, sink = mixed[0:number_of // 2 * 2:2], mixed[1:number_of // 2 * 2:2]
    margin = jnp.minimum(tallies[source_of] - 1, limit - tallies[sink]) // 2
    margin = jnp.where((source_of == ranking[0]) | (sink == ranking[0]) | (tallies[sink] == 0), 0, jnp.maximum(margin, 0))
    shifted = jax.random.randint(jax.random.fold_in(own, 4), (number_of // 2,), 0, 1 << 20) % (margin + 1)
    tallies = tallies.at[source_of].add(-shifted).at[sink].add(shifted)
    items = jnp.searchsorted(jnp.cumsum(tallies), jnp.arange(rows * top), side="right").astype(jnp.int32)
    listing = items.reshape(top, rows).T
    listing = listing[jax.random.permutation(jax.random.fold_in(own, 1), rows)]
    offset_by = jax.random.randint(jax.random.fold_in(own, 2), (rows, 1), 0, top)
    return jnp.take_along_axis(listing, (jnp.arange(top)[None, :] + offset_by) % top, axis=1)


def portions_of(amount, total, bound, lean, full):
    loads = [(1 << 20) // math.isqrt(grade ** lean) + 1 for grade in range(1, amount + 1)]
    largest = bound if full else min(bound, max(-(-total // amount), total * loads[0] // sum(loads)))
    least = 1 if total - largest >= amount - 1 else 0
    given, rest = [largest] + [least] * (amount - 1), total - largest - least * (amount - 1)
    while rest > 0:
        movable = [i for i in range(1, amount) if given[i] < largest] or [i for i in range(1, amount) if given[i] < bound]
        mass, budget = sum([loads[i] for i in movable]), rest
        for i in movable:
            addition = min(bound - given[i], max(1, budget * loads[i] // mass), rest)
            given[i] = given[i] + addition
            rest = rest - addition
    return np.array(given)


def gaussian(key, shape, spread, reach, cuts=(), held_as=jnp.bfloat16):
    drawn = jax.random.normal(key, shape, jnp.float32) * spread
    if len(cuts) > 0:
        drawn = block_scale(key, shape, cuts, -0.22, 0.18) * drawn
    return jnp.clip(drawn, min=-reach, max=reach).astype(held_as)


def setup_inputs(seed: int = 0) -> dict:
    splits = jax.random.split(jax.random.key(seed), 10)
    queries = draw_queries(jax.random.fold_in(splits[9], 71), 0)
    group_cond = gaussian(splits[1], (GROUPS, E), 0.7, 6.0, ((0, 8),))
    nbr_shard_keys = jax.random.split(jax.random.fold_in(splits[2], 1), GROUPS // GRP_DEV)
    nbr_shard_turns = jax.random.permutation(jax.random.fold_in(splits[2], 3), GROUPS // GRP_DEV)
    nbr_shard = jax.vmap(lambda own, number: assign_block(jax.random.fold_in(splits[2], 2), own, number, GRP_DEV, N_SEQ, K, CAP, 2))(nbr_shard_keys, nbr_shard_turns).reshape((GROUPS, K))
    nbr_row = touch_ends(jax.random.randint(splits[3], (GROUPS, K), 0, DB_DEV), jax.random.fold_in(splits[3], 1), 0, DB_DEV - 1).astype(jnp.int32)
    database = gaussian(splits[4], (DB_ROWS, NL, E), 1.0, 6.0, ((0, 8),))
    enc_gain = jnp.clip(1.0 + 0.15 * jax.random.normal(splits[5], (E,), jnp.float32), 0.25, 1.75).astype(jnp.bfloat16)
    w_in = gaussian(splits[6], (E_FF, E), E ** -0.5, 0.1875, ((0, 4),))
    w_out = gaussian(splits[7], (E_FF, E), E_FF ** -0.5, 0.125, ((0, 4),))
    w_kv = gaussian(splits[8], (2, E, HQ), E ** -0.5, 0.1875, ((1, 8), (2, 4)))
    return dict(queries=queries, group_cond=group_cond, nbr_shard=nbr_shard, nbr_row=nbr_row, database=database, enc_gain=enc_gain, w_in=w_in, w_out=w_out, w_kv=w_kv)


def attend_group(pieces):
    query_block, key_block, value_block = pieces
    scores = jnp.einsum('qhd,khd->hqk', query_block.astype(jnp.float32), key_block.astype(jnp.float32))
    scores = scores / jnp.sqrt(jnp.float32(HEAD))
    weights = jax.nn.softmax(scores, axis=-1).astype(jnp.bfloat16)
    weights = lax.optimization_barrier(weights).astype(jnp.float32)
    mixed = jnp.einsum('hqk,khd->qhd', weights, value_block.astype(jnp.float32))
    return mixed.astype(jnp.bfloat16)

def reference(queries, group_cond, nbr_shard, nbr_row, database, enc_gain, w_in, w_out, w_kv):
    flat_index = (nbr_shard * DB_DEV + nbr_row).astype(jnp.int32)
    rows = database[flat_index]
    summed = (rows.astype(jnp.float32) + group_cond.astype(jnp.float32)[:, None, None, :]).astype(jnp.bfloat16)
    flat_rows = summed.reshape(GROUPS * K * NL, E).astype(jnp.float32)
    mean_square = lax.optimization_barrier(jnp.mean(flat_rows * flat_rows, axis=1, keepdims=True))
    normed = (flat_rows * lax.rsqrt(mean_square + 1e-06) * enc_gain.astype(jnp.float32)).astype(jnp.bfloat16)
    pre_act = jnp.dot(normed, w_in.T, preferred_element_type=jnp.float32)
    hidden = jax.nn.gelu(pre_act).astype(jnp.bfloat16)
    ffn_out = jnp.dot(hidden, w_out, preferred_element_type=jnp.float32)
    encoded = (flat_rows + ffn_out).astype(jnp.bfloat16)
    keys = jnp.dot(encoded, w_kv[0], preferred_element_type=jnp.float32).astype(jnp.bfloat16)
    values = jnp.dot(encoded, w_kv[1], preferred_element_type=jnp.float32).astype(jnp.bfloat16)
    keys = keys.reshape(GROUPS, K * NL, HEADS_W, HEAD)
    values = values.reshape(GROUPS, K * NL, HEADS_W, HEAD)
    query_blocks = queries.reshape(GROUPS, GROUP, HEADS_W, HEAD)
    attended = lax.map(attend_group, (query_blocks, keys, values))
    return attended.reshape(TOKENS, HQ)
```

```python
import jax
import jax.numpy as jnp
from jax import lax
from jax.experimental import pallas as pl
from jax.experimental.pallas import tpu as pltpu
from jax.sharding import PartitionSpec as P

E = 896
HEAD = 128
GROUP = 64
K = 2
NL = 16


def slot_positions(shards, capacity):
    count = shards.shape[0]
    order = jnp.arange(count, dtype=jnp.int32)
    earlier = (shards[:, None] == shards[None, :]) & (order[None, :] < order[:, None])
    slot = jnp.sum(earlier.astype(jnp.int32), axis=1)
    return shards * capacity + slot


def request_table(positions, wanted, slot_total):
    match = positions[:, None] == jnp.arange(slot_total, dtype=jnp.int32)[None, :]
    return jnp.sum(jnp.where(match, wanted[:, None], 0), axis=0)


def body(queries, group_cond, nbr_shard, nbr_row, database, enc_gain, w_in, w_out, w_kv):
    seq_count = lax.axis_size("seq")
    group_count = nbr_shard.shape[0]
    capacity = (group_count * K + seq_count - 1) // seq_count
    slot_total = seq_count * capacity
    stored = database.shape[0]
    flat_shard = nbr_shard.reshape(-1)
    flat_row = nbr_row.reshape(-1)
    positions = slot_positions(flat_shard, capacity)
    table = request_table(positions, flat_row, slot_total).reshape(seq_count, capacity)
    store_flat = database.reshape(stored, NL * E)
    received = lax.all_to_all(table, "seq", split_axis=0, concat_axis=0, tiled=True)
    looked = jnp.take(store_flat, received.reshape(-1), axis=0)
    looked = looked.reshape(seq_count, received.shape[1], NL * E)
    replies = lax.all_to_all(looked, "seq", split_axis=0, concat_axis=0, tiled=True)
    raw_rows = jnp.take(replies.reshape(slot_total, NL * E), positions, axis=0)
    raw_rows = raw_rows.reshape(group_count, K, NL, E)
    summed_rows = (
        raw_rows.astype(jnp.float32) + group_cond.astype(jnp.float32)[:, None, None, :]
    ).astype(jnp.bfloat16)
    row_count = group_count * K * NL
    flat_rows = summed_rows.reshape(row_count, E).astype(jnp.float32)
    mean_square = jnp.mean(flat_rows * flat_rows, axis=1, keepdims=True)
    normed = (flat_rows * lax.rsqrt(mean_square + 1e-06) * enc_gain.astype(jnp.float32)).astype(
        jnp.bfloat16
    )
    pre_act = lax.dot_general(
        normed, w_in, (((1,), (1,)), ((), ())), preferred_element_type=jnp.float32
    )
    hidden = jax.nn.gelu(pre_act).astype(jnp.bfloat16)
    partial_out = jnp.dot(hidden, w_out, preferred_element_type=jnp.float32)
    ffn_out = lax.psum(partial_out, "tp")
    encoded = (flat_rows + ffn_out).astype(jnp.bfloat16)
    local_feat = w_kv.shape[2]
    piece = lax.all_gather(w_kv, "seq", axis=1, tiled=True)
    key_part = jnp.dot(encoded, piece[0], preferred_element_type=jnp.float32)
    value_part = jnp.dot(encoded, piece[1], preferred_element_type=jnp.float32)
    local_heads = local_feat // HEAD
    keys = key_part.astype(jnp.bfloat16).reshape(group_count, K * NL, local_heads, HEAD)
    values = value_part.astype(jnp.bfloat16).reshape(group_count, K * NL, local_heads, HEAD)
    query_blocks = queries.reshape(group_count, GROUP, local_heads, HEAD)
    scores = jnp.einsum("cqhd,ckhd->chqk", query_blocks, keys, preferred_element_type=jnp.float32)
    scores = scores / jnp.sqrt(jnp.float32(HEAD))
    weights = jax.nn.softmax(scores, axis=-1).astype(jnp.bfloat16)
    attended = jnp.einsum("chqk,ckhd->cqhd", weights, values, preferred_element_type=jnp.float32)
    return attended.astype(jnp.bfloat16).reshape(group_count * GROUP, local_feat)

MESH = pl.DeviceIdType.MESH
ACROSS = 4
PIECES = 8
WIDE = 256


def fused_kernel(
    queries_hbm, cond_ref, shard_ref, row_ref, db_ref, gain_ref, w_in_hbm, w_out_hbm, w_kv_ref,
    out_ref,
    wbuf, dbp, condf, xs, xv, nv, enc, part_send, part_recv, own_sum, y_send, y_recv,
    q_ref, w_in_ref, w_out_ref,
    local_sem, db_send, db_recv, w_send, w_recv, xs_send, xs_recv, sum_send, sum_recv,
):
    s = lax.axis_index("seq")
    t = lax.axis_index("tp")
    z, x = s // 2, s % 2
    core = t % 2
    flip = s + 1 - 2 * x
    sib = t + 1 - 2 * core
    ypeer = (t + 2) % 4
    stored = db_ref.shape[0]
    depth = w_kv_ref.shape[1]
    rows = enc.shape[0]
    half = rows // 2
    e = enc.shape[1]
    off = pl.multiple_of(jnp.minimum(t * WIDE, e - WIDE), 128)

    barrier = pltpu.get_barrier_semaphore()
    for i in range(1, 8):
        pl.semaphore_signal(barrier, inc=1, device_id=((s + i) % 8, t), device_id_type=MESH)
    pl.semaphore_signal(barrier, inc=1, device_id=(s, sib), device_id_type=MESH)
    pl.semaphore_signal(barrier, inc=1, device_id=(s, ypeer), device_id_type=MESH)
    loads = [
        pltpu.make_async_copy(w_in_hbm, w_in_ref, local_sem.at[0]),
        pltpu.make_async_copy(w_out_hbm, w_out_ref, local_sem.at[1]),
        pltpu.make_async_copy(queries_hbm, q_ref, local_sem.at[2]),
    ]
    for load in loads:
        load.start()
    pl.semaphore_wait(barrier, 9)

    def db_copy(i):
        return pltpu.make_async_remote_copy(
            src_ref=db_ref.at[:, :, pl.ds(off, WIDE)],
            dst_ref=dbp.at[pl.ds(s * stored, stored)],
            send_sem=db_send.at[i],
            recv_sem=db_recv.at[i],
            device_id=((s + i) % 8, t),
            device_id_type=MESH,
        )

    def db_arrival(i):
        source = (s + 8 - i) % 8
        return pltpu.make_async_copy(
            dbp.at[pl.ds(source * stored, stored)], dbp.at[pl.ds(source * stored, stored)], db_recv.at[i]
        )

    for i in range(1, 8):
        db_copy(i).start()

    def slot(p, b):
        return wbuf.at[p, pl.ds(pl.multiple_of(b * depth, 16), depth), :]

    def own_piece(p):
        return w_kv_ref.at[p % 2, :, pl.ds(pl.multiple_of((p // 2) * WIDE, WIDE), WIDE)]

    def w_copy(src, p, b, way):
        target = (flip, s + 2, s - 2)[way]
        return pltpu.make_async_remote_copy(
            src_ref=src,
            dst_ref=slot(p, b),
            send_sem=w_send.at[way, p, b],
            recv_sem=w_recv.at[p, b],
            device_id=(target, t),
            device_id_type=MESH,
        )

    def w_arrival(p, b):
        return pltpu.make_async_copy(slot(p, b), slot(p, b), w_recv.at[p, b])

    def own_start(p, carry):
        w_copy(own_piece(p), p, s, 0).start()

        @pl.when(z < ACROSS - 1)
        def _():
            w_copy(own_piece(p), p, s, 1).start()

        @pl.when(z > 0)
        def _():
            w_copy(own_piece(p), p, s, 2).start()

        pltpu.make_async_copy(own_piece(p), slot(p, s), w_recv.at[p, s]).start()
        return carry

    lax.fori_loop(0, PIECES, own_start, 0)

    def pass_on(hop, first, last):
        def one(p, carry):
            @pl.when(z >= hop)
            def _():
                b = s - 2 * hop
                w_arrival(p, b).wait()
                w_copy(slot(p, b), p, b, 0).start()

                @pl.when(z < ACROSS - 1)
                def _():
                    w_copy(slot(p, b), p, b, 1).start()

            @pl.when(z + hop < ACROSS)
            def _():
                b = s + 2 * hop
                w_arrival(p, b).wait()
                w_copy(slot(p, b), p, b, 0).start()

                @pl.when(z > 0)
                def _():
                    w_copy(slot(p, b), p, b, 2).start()

            return carry

        lax.fori_loop(first, last, one, 0)

    condf[...] = cond_ref[:, pl.ds(off, WIDE)].astype(jnp.float32)
    dbp[pl.ds(s * stored, stored)] = db_ref[:, :, pl.ds(off, WIDE)]
    for i in range(1, 8):
        db_arrival(i).wait()

    def pick(g, carry):
        for k in range(K):
            at = shard_ref[g, k] * stored + row_ref[g, k]
            picked = dbp[at].astype(jnp.float32) + condf[pl.ds(g, 1), :]
            xs[t, pl.ds(pl.multiple_of((g * K + k) * NL, NL), NL), :] = picked.astype(jnp.bfloat16)
        return carry

    lax.fori_loop(0, rows // (K * NL), pick, 0)

    def xs_copy(quarter, target, number):
        return pltpu.make_async_remote_copy(
            src_ref=xs.at[quarter],
            dst_ref=xs.at[quarter],
            send_sem=xs_send.at[number],
            recv_sem=xs_recv.at[quarter],
            device_id=(s, target),
            device_id_type=MESH,
        )

    def xs_arrival(quarter):
        return pltpu.make_async_copy(xs.at[quarter], xs.at[quarter], xs_recv.at[quarter])

    xs_copy(t, ypeer, 0).start()
    xs_copy(t, sib, 1).start()
    pass_on(1, 0, PIECES // 2)
    xs_arrival(ypeer).wait()
    xs_copy(ypeer, sib, 2).start()
    pass_on(1, PIECES // 2, PIECES)
    xs_arrival(sib).wait()
    xs_arrival((sib + 2) % 4).wait()

    gain = gain_ref[...].astype(jnp.float32)

    def norm(i, carry):
        at = pl.ds(pl.multiple_of(i * 64, 64), 64)
        whole = jnp.concatenate(
            [xs[0, at, :], xs[1, at, :], xs[2, at, :], xs[3, at, pl.ds(4 * WIDE - e, e - 3 * WIDE)]], axis=1
        )
        xv[at, :] = whole
        wide = whole.astype(jnp.float32)
        mean_square = jnp.mean(wide * wide, axis=1, keepdims=True)
        nv[at, :] = (wide * lax.rsqrt(mean_square + 1e-06) * gain).astype(jnp.bfloat16)
        return carry

    lax.fori_loop(0, rows // 64, norm, 0)
    loads[0].wait()
    loads[1].wait()

    def ffn(first):
        block = nv[pl.ds(pl.multiple_of(first, 128), 128), :]
        pre_act = lax.dot_general(
            block, w_in_ref[...], (((1,), (1,)), ((), ())), preferred_element_type=jnp.float32
        )
        hidden = jax.nn.gelu(pre_act).astype(jnp.bfloat16)
        return jnp.dot(hidden, w_out_ref[...], preferred_element_type=jnp.float32)

    def sum_copy(src, dst, target, number):
        return pltpu.make_async_remote_copy(
            src_ref=src,
            dst_ref=dst,
            send_sem=sum_send.at[number],
            recv_sem=sum_recv.at[number],
            device_id=(s, target),
            device_id_type=MESH,
        )

    theirs = (1 - core) * half
    mine = core * half
    steps = half // 128

    def at_row(i):
        return pl.ds(pl.multiple_of(i * 128, 128), 128)

    def to_sib(i):
        return sum_copy(part_send.at[at_row(i)], part_recv.at[at_row(i)], sib, i)

    def to_y(i):
        return sum_copy(y_send.at[at_row(i)], y_recv.at[at_row(i)], ypeer, steps + i)

    def to_share(i):
        where = pl.ds(pl.multiple_of(mine + i * 128, 128), 128)
        return sum_copy(enc.at[where], enc.at[where], sib, 2 * steps + i)

    def share_arrival(i):
        where = pl.ds(pl.multiple_of(theirs + i * 128, 128), 128)
        return pltpu.make_async_copy(enc.at[where], enc.at[where], sum_recv.at[2 * steps + i])

    def send_theirs(i, carry):
        part_send[at_row(i), :] = ffn(theirs + i * 128).astype(jnp.bfloat16)
        to_sib(i).start()
        return carry

    lax.fori_loop(0, steps, send_theirs, 0)

    def send_mine(i, carry):
        own = ffn(mine + i * 128)
        to_sib(i).wait_recv()
        own = own + part_recv[at_row(i), :].astype(jnp.float32)
        own_sum[at_row(i), :] = own
        y_send[at_row(i), :] = own.astype(jnp.bfloat16)
        to_y(i).start()
        return carry

    lax.fori_loop(0, steps, send_mine, 0)
    pass_on(2, 0, PIECES)

    def share_mine(i, carry):
        where = pl.ds(pl.multiple_of(mine + i * 128, 128), 128)
        to_y(i).wait_recv()
        total = own_sum[at_row(i), :] + y_recv[at_row(i), :].astype(jnp.float32)
        enc[where, :] = (xv[where, :].astype(jnp.float32) + total).astype(jnp.bfloat16)
        to_share(i).start()
        return carry

    lax.fori_loop(0, steps, share_mine, 0)
    pass_on(3, 0, PIECES)

    def await_share(i, carry):
        share_arrival(i).wait()
        return carry

    lax.fori_loop(0, steps, await_share, 0)
    loads[2].wait()

    span = 4 * K * NL
    qspan = 4 * GROUP
    tall = lax.broadcasted_iota(jnp.int32, (qspan, span), 0) // GROUP
    flat = lax.broadcasted_iota(jnp.int32, (qspan, span), 1) // (K * NL)
    inside = tall == flat
    scale = HEAD ** -0.5
    ones = jnp.ones((span, HEAD), jnp.bfloat16)

    def chunk(c, carry):
        for j in range(2):
            p = 2 * c + j
            pltpu.make_async_copy(own_piece(p), slot(p, s), w_recv.at[p, s]).wait()
            for i in range(ACROSS):
                w_arrival(p, 2 * i + 1 - x).wait()

        def quad(i, inner):
            krows = pl.ds(pl.multiple_of(i * span, span), span)
            qrows = pl.ds(pl.multiple_of(i * qspan, qspan), qspan)
            block = enc[krows, :]
            keys = jnp.dot(block, wbuf[2 * c], preferred_element_type=jnp.float32).astype(jnp.bfloat16)
            values = jnp.dot(block, wbuf[2 * c + 1], preferred_element_type=jnp.float32).astype(jnp.bfloat16)
            for h in range(WIDE // HEAD):
                cols = pl.ds(pl.multiple_of(c * WIDE + h * HEAD, HEAD), HEAD)
                query = q_ref[qrows, cols]
                scores = lax.dot_general(
                    query, keys[:, h * HEAD : (h + 1) * HEAD], (((1,), (1,)), ((), ())),
                    preferred_element_type=jnp.float32,
                )
                scores = jnp.where(inside, scores * scale, -jnp.inf)
                top = jnp.max(scores, axis=1, keepdims=True)
                grown = jnp.exp(scores - top).astype(jnp.bfloat16)
                both = jnp.concatenate([values[:, h * HEAD : (h + 1) * HEAD], ones], axis=1)
                mixed = jnp.dot(grown, both, preferred_element_type=jnp.float32)
                out_ref[qrows, cols] = (mixed[:, :HEAD] / mixed[:, HEAD:]).astype(jnp.bfloat16)
            return inner

        lax.fori_loop(0, rows // span, quad, 0)
        return carry

    lax.fori_loop(0, PIECES // 2, chunk, 0)

    for i in range(1, 8):
        db_copy(i).wait_send()
    xs_copy(t, ypeer, 0).wait_send()
    xs_copy(t, sib, 1).wait_send()
    xs_copy(ypeer, sib, 2).wait_send()

    def sums_done(i, carry):
        to_sib(i).wait_send()
        to_y(i).wait_send()
        to_share(i).wait_send()
        return carry

    lax.fori_loop(0, steps, sums_done, 0)

    def sends_done(p, carry):
        w_copy(own_piece(p), p, s, 0).wait_send()

        @pl.when(z < ACROSS - 1)
        def _():
            w_copy(own_piece(p), p, s, 1).wait_send()

        @pl.when(z > 0)
        def _():
            w_copy(own_piece(p), p, s, 2).wait_send()

        for hop in range(1, ACROSS):
            @pl.when(z >= hop)
            def _():
                b = s - 2 * hop
                w_copy(slot(p, b), p, b, 0).wait_send()

                @pl.when(z < ACROSS - 1)
                def _():
                    w_copy(slot(p, b), p, b, 1).wait_send()

            @pl.when(z + hop < ACROSS)
            def _():
                b = s + 2 * hop
                w_copy(slot(p, b), p, b, 0).wait_send()

                @pl.when(z > 0)
                def _():
                    w_copy(slot(p, b), p, b, 2).wait_send()

        return carry

    lax.fori_loop(0, PIECES, sends_done, 0)


def fused_body(queries, group_cond, nbr_shard, nbr_row, database, enc_gain, w_in, w_out, w_kv):
    bf16, f32 = jnp.bfloat16, jnp.float32
    rows = nbr_shard.shape[0] * K * NL
    half = rows // 2
    steps = half // 128
    vmem = pl.BlockSpec(memory_space=pltpu.VMEM)
    smem = pl.BlockSpec(memory_space=pltpu.SMEM)
    anywhere = pl.BlockSpec(memory_space=pl.ANY)
    dma = pltpu.SemaphoreType.DMA
    return pl.pallas_call(
        fused_kernel,
        out_shape=jax.ShapeDtypeStruct(queries.shape, bf16),
        in_specs=[anywhere, vmem, smem, smem, vmem, vmem, anywhere, anywhere, vmem],
        out_specs=vmem,
        scratch_shapes=[
            pltpu.VMEM((PIECES, E, WIDE), bf16),
            pltpu.VMEM((8 * database.shape[0], NL, WIDE), bf16),
            pltpu.VMEM((group_cond.shape[0], WIDE), f32),
            pltpu.VMEM((4, rows, WIDE), bf16),
            pltpu.VMEM((rows, E), bf16),
            pltpu.VMEM((rows, E), bf16),
            pltpu.VMEM((rows, E), bf16),
            pltpu.VMEM((half, E), bf16),
            pltpu.VMEM((half, E), bf16),
            pltpu.VMEM((half, E), f32),
            pltpu.VMEM((half, E), bf16),
            pltpu.VMEM((half, E), bf16),
            pltpu.VMEM(queries.shape, bf16),
            pltpu.VMEM(w_in.shape, bf16),
            pltpu.VMEM(w_out.shape, bf16),
            dma((3,)),
            dma((8,)),
            dma((8,)),
            dma((3, PIECES, 8)),
            dma((PIECES, 8)),
            dma((3,)),
            dma((4,)),
            dma((3 * steps,)),
            dma((3 * steps,)),
        ],
        compiler_params=pltpu.CompilerParams(
            collective_id=0, has_side_effects=True, vmem_limit_bytes=40 * 1024 * 1024
        ),
    )(queries, group_cond, nbr_shard, nbr_row, database, enc_gain.reshape(1, E), w_in, w_out, w_kv)


def solution(mesh):
    placed = (
        P("seq", "tp"),
        P("seq", None),
        P("seq", None),
        P("seq", None),
        P("seq", None, None),
        P(),
        P("tp", None),
        P("tp", None),
        P(None, "seq", "tp"),
    )
    fused = mesh.shape["seq"] == 8 and mesh.shape["tp"] == 4
    return jax.shard_map(
        fused_body if fused else body, mesh=mesh, in_specs=placed, out_specs=P("seq", "tp"), check_vma=False
    )
```

```python
import jax
import jax.numpy as jnp
from jax import lax
from jax.experimental import pallas as pl
from jax.experimental.pallas import tpu as pltpu
from jax.sharding import PartitionSpec as P

E = 896
HEAD = 128
GROUP = 64
K = 2
NL = 16


def slot_positions(shards, capacity):
    count = shards.shape[0]
    order = jnp.arange(count, dtype=jnp.int32)
    earlier = (shards[:, None] == shards[None, :]) & (order[None, :] < order[:, None])
    slot = jnp.sum(earlier.astype(jnp.int32), axis=1)
    return shards * capacity + slot


def request_table(positions, wanted, slot_total):
    match = positions[:, None] == jnp.arange(slot_total, dtype=jnp.int32)[None, :]
    return jnp.sum(jnp.where(match, wanted[:, None], 0), axis=0)


def body(queries, group_cond, nbr_shard, nbr_row, database, enc_gain, w_in, w_out, w_kv):
    seq_count = lax.axis_size("seq")
    group_count = nbr_shard.shape[0]
    capacity = (group_count * K + seq_count - 1) // seq_count
    slot_total = seq_count * capacity
    stored = database.shape[0]
    flat_shard = nbr_shard.reshape(-1)
    flat_row = nbr_row.reshape(-1)
    positions = slot_positions(flat_shard, capacity)
    table = request_table(positions, flat_row, slot_total).reshape(seq_count, capacity)
    store_flat = database.reshape(stored, NL * E)
    received = lax.all_to_all(table, "seq", split_axis=0, concat_axis=0, tiled=True)
    looked = jnp.take(store_flat, received.reshape(-1), axis=0)
    looked = looked.reshape(seq_count, received.shape[1], NL * E)
    replies = lax.all_to_all(looked, "seq", split_axis=0, concat_axis=0, tiled=True)
    raw_rows = jnp.take(replies.reshape(slot_total, NL * E), positions, axis=0)
    raw_rows = raw_rows.reshape(group_count, K, NL, E)
    summed_rows = (
        raw_rows.astype(jnp.float32) + group_cond.astype(jnp.float32)[:, None, None, :]
    ).astype(jnp.bfloat16)
    row_count = group_count * K * NL
    flat_rows = summed_rows.reshape(row_count, E).astype(jnp.float32)
    mean_square = jnp.mean(flat_rows * flat_rows, axis=1, keepdims=True)
    normed = (flat_rows * lax.rsqrt(mean_square + 1e-06) * enc_gain.astype(jnp.float32)).astype(
        jnp.bfloat16
    )
    pre_act = lax.dot_general(
        normed, w_in, (((1,), (1,)), ((), ())), preferred_element_type=jnp.float32
    )
    hidden = jax.nn.gelu(pre_act).astype(jnp.bfloat16)
    partial_out = jnp.dot(hidden, w_out, preferred_element_type=jnp.float32)
    ffn_out = lax.psum(partial_out, "tp")
    encoded = (flat_rows + ffn_out).astype(jnp.bfloat16)
    local_feat = w_kv.shape[2]
    piece = lax.all_gather(w_kv, "seq", axis=1, tiled=True)
    key_part = jnp.dot(encoded, piece[0], preferred_element_type=jnp.float32)
    value_part = jnp.dot(encoded, piece[1], preferred_element_type=jnp.float32)
    local_heads = local_feat // HEAD
    keys = key_part.astype(jnp.bfloat16).reshape(group_count, K * NL, local_heads, HEAD)
    values = value_part.astype(jnp.bfloat16).reshape(group_count, K * NL, local_heads, HEAD)
    query_blocks = queries.reshape(group_count, GROUP, local_heads, HEAD)
    scores = jnp.einsum("cqhd,ckhd->chqk", query_blocks, keys, preferred_element_type=jnp.float32)
    scores = scores / jnp.sqrt(jnp.float32(HEAD))
    weights = jax.nn.softmax(scores, axis=-1).astype(jnp.bfloat16)
    attended = jnp.einsum("chqk,ckhd->cqhd", weights, values, preferred_element_type=jnp.float32)
    return attended.astype(jnp.bfloat16).reshape(group_count * GROUP, local_feat)

MESH = pl.DeviceIdType.MESH
ACROSS = 4
PIECES = 8
WIDE = 256


def fused_kernel(
    queries_hbm, cond_hbm, shard_ref, row_ref, db_ref, gain_hbm, w_in_hbm, w_out_hbm, w_kv_ref,
    out_ref,
    wbuf, dbp, cond_ref, gain_ref, condf, xs, xv, keys, values, enc, part_send, part_recv, own_sum, y_send, y_recv,
    q_ref, w_in_ref, w_out_ref,
    local_sem, db_send, db_recv, w_send, w_recv, xs_send, xs_recv, sum_send, sum_recv,
):
    s = lax.axis_index("seq")
    t = lax.axis_index("tp")
    z, x = s // 2, s % 2
    core = t % 2
    flip = s + 1 - 2 * x
    sib = t + 1 - 2 * core
    ypeer = (t + 2) % 4
    stored = db_ref.shape[0]
    depth = w_kv_ref.shape[1]
    rows = enc.shape[0]
    e = enc.shape[1]
    off = pl.multiple_of(jnp.minimum(t * WIDE, e - WIDE), 128)

    barrier = pltpu.get_barrier_semaphore()
    for i in range(1, 8):
        pl.semaphore_signal(barrier, inc=1, device_id=((s + i) % 8, t), device_id_type=MESH)
    pl.semaphore_signal(barrier, inc=1, device_id=(s, sib), device_id_type=MESH)
    pl.semaphore_signal(barrier, inc=1, device_id=(s, ypeer), device_id_type=MESH)
    loads = [
        pltpu.make_async_copy(w_in_hbm, w_in_ref, local_sem.at[0]),
        pltpu.make_async_copy(w_out_hbm, w_out_ref, local_sem.at[1]),
        pltpu.make_async_copy(queries_hbm, q_ref, local_sem.at[2]),
        pltpu.make_async_copy(gain_hbm, gain_ref, local_sem.at[3]),
        pltpu.make_async_copy(cond_hbm.at[:, pl.ds(off, WIDE)], cond_ref, local_sem.at[4]),
        pltpu.make_async_copy(
            db_ref.at[:, :, pl.ds(off, WIDE)], dbp.at[pl.ds(s * stored, stored)], local_sem.at[5]
        ),
    ]
    for load in loads:
        load.start()
    pl.semaphore_wait(barrier, 9)

    def db_copy(i):
        return pltpu.make_async_remote_copy(
            src_ref=db_ref.at[:, :, pl.ds(off, WIDE)],
            dst_ref=dbp.at[pl.ds(s * stored, stored)],
            send_sem=db_send.at[i],
            recv_sem=db_recv.at[i],
            device_id=((s + i) % 8, t),
            device_id_type=MESH,
        )

    def db_arrival(i):
        source = (s + 8 - i) % 8
        return pltpu.make_async_copy(
            dbp.at[pl.ds(source * stored, stored)], dbp.at[pl.ds(source * stored, stored)], db_recv.at[i]
        )

    for i in range(1, 8):
        db_copy(i).start()

    def slot(p, b):
        return wbuf.at[p, pl.ds(pl.multiple_of(b * depth, 16), depth), :]

    def own_piece(p):
        return w_kv_ref.at[p % 2, :, pl.ds(pl.multiple_of((p // 2) * WIDE, WIDE), WIDE)]

    def w_copy(src, p, b, way):
        target = (flip, s + 2, s - 2)[way]
        return pltpu.make_async_remote_copy(
            src_ref=src,
            dst_ref=slot(p, b),
            send_sem=w_send.at[way, p, b],
            recv_sem=w_recv.at[p, b],
            device_id=(target, t),
            device_id_type=MESH,
        )

    def w_arrival(p, b):
        return pltpu.make_async_copy(slot(p, b), slot(p, b), w_recv.at[p, b])

    def own_start(p, carry):
        w_copy(own_piece(p), p, s, 0).start()

        @pl.when(z < ACROSS - 1)
        def _():
            w_copy(own_piece(p), p, s, 1).start()

        @pl.when(z > 0)
        def _():
            w_copy(own_piece(p), p, s, 2).start()

        pltpu.make_async_copy(own_piece(p), slot(p, s), w_recv.at[p, s]).start()
        return carry

    lax.fori_loop(0, PIECES, own_start, 0)

    def pass_on(hop, first, last):
        def one(p, carry):
            @pl.when(z >= hop)
            def _():
                b = s - 2 * hop
                w_arrival(p, b).wait()
                w_copy(slot(p, b), p, b, 0).start()

                @pl.when(z < ACROSS - 1)
                def _():
                    w_copy(slot(p, b), p, b, 1).start()

            @pl.when(z + hop < ACROSS)
            def _():
                b = s + 2 * hop
                w_arrival(p, b).wait()
                w_copy(slot(p, b), p, b, 0).start()

                @pl.when(z > 0)
                def _():
                    w_copy(slot(p, b), p, b, 2).start()

            return carry

        lax.fori_loop(first, last, one, 0)

    for load in loads[3:]:
        load.wait()
    condf[...] = cond_ref[...].astype(jnp.float32)
    for i in range(1, 8):
        db_arrival(i).wait()

    blocks = rows // 128

    def at_row(i):
        return pl.ds(i * 128, 128)

    def xs_copy(quarter, r, target, number):
        return pltpu.make_async_remote_copy(
            src_ref=xs.at[quarter, at_row(r)],
            dst_ref=xs.at[quarter, at_row(r)],
            send_sem=xs_send.at[number, r],
            recv_sem=xs_recv.at[quarter, r],
            device_id=(s, target),
            device_id_type=MESH,
        )

    def xs_arrival(quarter, r):
        here = xs.at[quarter, at_row(r)]
        return pltpu.make_async_copy(here, here, xs_recv.at[quarter, r])

    def pick(g, carry):
        for k in range(K):
            at = shard_ref[k, g] * stored + row_ref[k, g]
            picked = dbp[at].astype(jnp.float32) + condf[pl.ds(g, 1), :]
            xs[t, pl.ds(pl.multiple_of((g * K + k) * NL, NL), NL), :] = picked.astype(jnp.bfloat16)
        return carry

    per_block = 128 // (K * NL)
    for r in range(blocks):
        lax.fori_loop(r * per_block, (r + 1) * per_block, pick, 0)
        xs_copy(t, r, ypeer, 0).start()
        xs_copy(t, r, sib, 1).start()

    gain = gain_ref[...].astype(jnp.float32).reshape(1, e)
    theirs = (1 - core) * 64
    mine = core * 64

    def rows_of(r, inner):
        return pl.ds(pl.multiple_of(r * 128 + inner, 64), 64)

    def sum_copy(src, dst, target, number, r):
        return pltpu.make_async_remote_copy(
            src_ref=src,
            dst_ref=dst,
            send_sem=sum_send.at[number, r],
            recv_sem=sum_recv.at[number, r],
            device_id=(s, target),
            device_id_type=MESH,
        )

    def to_sib(r):
        return sum_copy(part_send.at[r], part_recv.at[r], sib, 0, r)

    def to_y(r):
        return sum_copy(y_send.at[r], y_recv.at[r], ypeer, 1, r)

    def to_share(r):
        return sum_copy(enc.at[rows_of(r, mine)], enc.at[rows_of(r, mine)], sib, 2, r)

    def share_arrival(r):
        here = enc.at[rows_of(r, theirs)]
        return pltpu.make_async_copy(here, here, sum_recv.at[2, r])

    def relay(r):
        xs_arrival(ypeer, r).wait()
        xs_copy(ypeer, r, sib, 2).start()

    def feed_forward(r):
        xs_arrival(sib, r).wait()
        xs_arrival((sib + 2) % 4, r).wait()
        at = at_row(r)
        whole = jnp.concatenate(
            [xs[0, at, :], xs[1, at, :], xs[2, at, :], xs[3, at, pl.ds(4 * WIDE - e, e - 3 * WIDE)]], axis=1
        )
        xv[at, :] = whole
        wide = whole.astype(jnp.float32)
        mean_square = jnp.mean(wide * wide, axis=1, keepdims=True)
        normed = (wide * lax.rsqrt(mean_square + 1e-06) * gain).astype(jnp.bfloat16)
        pre_act = lax.dot_general(
            normed, w_in_ref[...], (((1,), (1,)), ((), ())), preferred_element_type=jnp.float32
        )
        hidden = jax.nn.gelu(pre_act).astype(jnp.bfloat16)
        own_sum[at, :] = jnp.dot(hidden, w_out_ref[...], preferred_element_type=jnp.float32)
        part_send[r] = own_sum[rows_of(r, theirs), :].astype(jnp.bfloat16)
        to_sib(r).start()

    def add_sib(r):
        to_sib(r).wait_recv()
        own = own_sum[rows_of(r, mine), :] + part_recv[r].astype(jnp.float32)
        own_sum[rows_of(r, mine), :] = own
        y_send[r] = own.astype(jnp.bfloat16)
        to_y(r).start()

    def share(r):
        to_y(r).wait_recv()
        where = rows_of(r, mine)
        total = own_sum[where, :] + y_recv[r].astype(jnp.float32)
        enc[where, :] = (xv[where, :].astype(jnp.float32) + total).astype(jnp.bfloat16)
        to_share(r).start()

    loads[0].wait()
    loads[1].wait()
    relay(0)
    for r in range(blocks):
        if r + 1 < blocks:
            relay(r + 1)
        feed_forward(r)
        if r:
            add_sib(r - 1)
        pass_on(1, 2 * r, 2 * r + 2)
    add_sib(blocks - 1)
    for r in range(blocks):
        pass_on(2, 2 * r, 2 * r + 2)
        share(r)
    pass_on(3, 0, 4)
    for r in range(blocks):
        share_arrival(r).wait()
    loads[2].wait()

    span = 4 * K * NL
    qspan = 4 * GROUP
    tall = lax.broadcasted_iota(jnp.int32, (qspan, span), 0) // GROUP
    flat = lax.broadcasted_iota(jnp.int32, (qspan, span), 1) // (K * NL)
    inside = tall == flat
    scale = HEAD ** -0.5 * 1.4426950408889634
    ones = jnp.ones((span, HEAD), jnp.bfloat16)

    def chunk(c, carry):
        for j in range(2):
            p = 2 * c + j
            pltpu.make_async_copy(own_piece(p), slot(p, s), w_recv.at[p, s]).wait()

            for i in range(ACROSS):
                w_arrival(p, 2 * i + 1 - x).wait()

        pass_on(3, jnp.minimum(2 * c + 4, PIECES), jnp.minimum(2 * c + 6, PIECES))
        block = enc[...]
        keys[...] = jnp.dot(block, wbuf[2 * c], preferred_element_type=jnp.float32).astype(jnp.bfloat16)
        values[...] = jnp.dot(block, wbuf[2 * c + 1], preferred_element_type=jnp.float32).astype(jnp.bfloat16)
        for h in range(WIDE // HEAD):
            cols = pl.ds(pl.multiple_of(c * WIDE + h * HEAD, HEAD), HEAD)
            part = slice(h * HEAD, (h + 1) * HEAD)
            for i in range(rows // span):
                krows = slice(i * span, (i + 1) * span)
                qrows = slice(i * qspan, (i + 1) * qspan)
                scores = lax.dot_general(
                    q_ref[qrows, cols], keys[krows, part], (((1,), (1,)), ((), ())),
                    preferred_element_type=jnp.float32,
                )
                scores = jnp.where(inside, scores * scale, -jnp.inf)
                top = jnp.max(scores, axis=1, keepdims=True)
                grown = jnp.exp2(scores - top).astype(jnp.bfloat16)
                both = jnp.concatenate([values[krows, part], ones], axis=1)
                mixed = jnp.dot(grown, both, preferred_element_type=jnp.float32)
                out_ref[qrows, cols] = (mixed[:, :HEAD] / mixed[:, HEAD:]).astype(jnp.bfloat16)
        return carry

    lax.fori_loop(0, PIECES // 2, chunk, 0)

    for i in range(1, 8):
        db_copy(i).wait_send()
    for r in range(blocks):
        xs_copy(t, r, ypeer, 0).wait_send()
        xs_copy(t, r, sib, 1).wait_send()
        xs_copy(ypeer, r, sib, 2).wait_send()
        to_sib(r).wait_send()
        to_y(r).wait_send()
        to_share(r).wait_send()

    def sends_done(p, carry):
        w_copy(own_piece(p), p, s, 0).wait_send()

        @pl.when(z < ACROSS - 1)
        def _():
            w_copy(own_piece(p), p, s, 1).wait_send()

        @pl.when(z > 0)
        def _():
            w_copy(own_piece(p), p, s, 2).wait_send()

        @pl.when(p >= 0)
        def _():
            for hop in range(1, ACROSS):
                @pl.when(z >= hop)
                def _():
                    b = s - 2 * hop
                    w_copy(slot(p, b), p, b, 0).wait_send()

                    @pl.when(z < ACROSS - 1)
                    def _():
                        w_copy(slot(p, b), p, b, 1).wait_send()

                @pl.when(z + hop < ACROSS)
                def _():
                    b = s + 2 * hop
                    w_copy(slot(p, b), p, b, 0).wait_send()

                    @pl.when(z > 0)
                    def _():
                        w_copy(slot(p, b), p, b, 2).wait_send()

        return carry

    lax.fori_loop(0, PIECES, sends_done, 0)


def fused_body(queries, group_cond, nbr_shard, nbr_row, database, enc_gain, w_in, w_out, w_kv):
    bf16, f32 = jnp.bfloat16, jnp.float32
    rows = nbr_shard.shape[0] * K * NL
    blocks = rows // 128
    vmem = pl.BlockSpec(memory_space=pltpu.VMEM)
    smem = pl.BlockSpec(memory_space=pltpu.SMEM)
    hbm = pl.BlockSpec(memory_space=pltpu.HBM)
    dma = pltpu.SemaphoreType.DMA
    return pl.pallas_call(
        fused_kernel,
        out_shape=jax.ShapeDtypeStruct(queries.shape, bf16),
        in_specs=[hbm, hbm, smem, smem, hbm, hbm, hbm, hbm, hbm],
        out_specs=vmem,
        scratch_shapes=[
            pltpu.VMEM((PIECES, E, WIDE), bf16),
            pltpu.VMEM((8 * database.shape[0], NL, WIDE), bf16),
            pltpu.VMEM((group_cond.shape[0], WIDE), bf16),
            pltpu.VMEM(enc_gain.shape, bf16),
            pltpu.VMEM((group_cond.shape[0], WIDE), f32),
            pltpu.VMEM((4, rows, WIDE), bf16),
            pltpu.VMEM((rows, E), bf16),
            pltpu.VMEM((rows, WIDE), bf16),
            pltpu.VMEM((rows, WIDE), bf16),
            pltpu.VMEM((rows, E), bf16),
            pltpu.VMEM((blocks, 64, E), bf16),
            pltpu.VMEM((blocks, 64, E), bf16),
            pltpu.VMEM((rows, E), f32),
            pltpu.VMEM((blocks, 64, E), bf16),
            pltpu.VMEM((blocks, 64, E), bf16),
            pltpu.VMEM(queries.shape, bf16),
            pltpu.VMEM(w_in.shape, bf16),
            pltpu.VMEM(w_out.shape, bf16),
            dma((6,)),
            dma((8,)),
            dma((8,)),
            dma((3, PIECES, 8)),
            dma((PIECES, 8)),
            dma((3, blocks)),
            dma((4, blocks)),
            dma((3, blocks)),
            dma((3, blocks)),
        ],
        compiler_params=pltpu.CompilerParams(
            collective_id=0, has_side_effects=True, vmem_limit_bytes=62 * 1024 * 1024
        ),
    )(queries, group_cond, nbr_shard.T, nbr_row.T, database, enc_gain, w_in, w_out, w_kv)


def solution(mesh):
    placed = (
        P("seq", "tp"),
        P("seq", None),
        P("seq", None),
        P("seq", None),
        P("seq", None, None),
        P(),
        P("tp", None),
        P("tp", None),
        P(None, "seq", "tp"),
    )
    fused = mesh.shape["seq"] == 8 and mesh.shape["tp"] == 4
    return jax.shard_map(
        fused_body if fused else body, mesh=mesh, in_specs=placed, out_specs=P("seq", "tp"), check_vma=False
    )
```

```python
import jax
import jax.numpy as jnp
from jax import lax
from jax.experimental import pallas as pl
from jax.experimental.pallas import tpu as pltpu
from jax.sharding import PartitionSpec as P

E = 896
HEAD = 128
GROUP = 64
K = 2
NL = 16


def slot_positions(shards, capacity):
    count = shards.shape[0]
    order = jnp.arange(count, dtype=jnp.int32)
    earlier = (shards[:, None] == shards[None, :]) & (order[None, :] < order[:, None])
    slot = jnp.sum(earlier.astype(jnp.int32), axis=1)
    return shards * capacity + slot


def request_table(positions, wanted, slot_total):
    match = positions[:, None] == jnp.arange(slot_total, dtype=jnp.int32)[None, :]
    return jnp.sum(jnp.where(match, wanted[:, None], 0), axis=0)


def body(queries, group_cond, nbr_shard, nbr_row, database, enc_gain, w_in, w_out, w_kv):
    seq_count = lax.axis_size("seq")
    group_count = nbr_shard.shape[0]
    capacity = (group_count * K + seq_count - 1) // seq_count
    slot_total = seq_count * capacity
    stored = database.shape[0]
    flat_shard = nbr_shard.reshape(-1)
    flat_row = nbr_row.reshape(-1)
    positions = slot_positions(flat_shard, capacity)
    table = request_table(positions, flat_row, slot_total).reshape(seq_count, capacity)
    store_flat = database.reshape(stored, NL * E)
    received = lax.all_to_all(table, "seq", split_axis=0, concat_axis=0, tiled=True)
    looked = jnp.take(store_flat, received.reshape(-1), axis=0)
    looked = looked.reshape(seq_count, received.shape[1], NL * E)
    replies = lax.all_to_all(looked, "seq", split_axis=0, concat_axis=0, tiled=True)
    raw_rows = jnp.take(replies.reshape(slot_total, NL * E), positions, axis=0)
    raw_rows = raw_rows.reshape(group_count, K, NL, E)
    summed_rows = (
        raw_rows.astype(jnp.float32) + group_cond.astype(jnp.float32)[:, None, None, :]
    ).astype(jnp.bfloat16)
    row_count = group_count * K * NL
    flat_rows = summed_rows.reshape(row_count, E).astype(jnp.float32)
    mean_square = jnp.mean(flat_rows * flat_rows, axis=1, keepdims=True)
    normed = (flat_rows * lax.rsqrt(mean_square + 1e-06) * enc_gain.astype(jnp.float32)).astype(
        jnp.bfloat16
    )
    pre_act = lax.dot_general(
        normed, w_in, (((1,), (1,)), ((), ())), preferred_element_type=jnp.float32
    )
    hidden = jax.nn.gelu(pre_act).astype(jnp.bfloat16)
    partial_out = jnp.dot(hidden, w_out, preferred_element_type=jnp.float32)
    ffn_out = lax.psum(partial_out, "tp")
    encoded = (flat_rows + ffn_out).astype(jnp.bfloat16)
    local_feat = w_kv.shape[2]
    piece = lax.all_gather(w_kv, "seq", axis=1, tiled=True)
    key_part = jnp.dot(encoded, piece[0], preferred_element_type=jnp.float32)
    value_part = jnp.dot(encoded, piece[1], preferred_element_type=jnp.float32)
    local_heads = local_feat // HEAD
    keys = key_part.astype(jnp.bfloat16).reshape(group_count, K * NL, local_heads, HEAD)
    values = value_part.astype(jnp.bfloat16).reshape(group_count, K * NL, local_heads, HEAD)
    query_blocks = queries.reshape(group_count, GROUP, local_heads, HEAD)
    scores = jnp.einsum("cqhd,ckhd->chqk", query_blocks, keys, preferred_element_type=jnp.float32)
    scores = scores / jnp.sqrt(jnp.float32(HEAD))
    weights = jax.nn.softmax(scores, axis=-1).astype(jnp.bfloat16)
    attended = jnp.einsum("chqk,ckhd->cqhd", weights, values, preferred_element_type=jnp.float32)
    return attended.astype(jnp.bfloat16).reshape(group_count * GROUP, local_feat)

MESH = pl.DeviceIdType.MESH
ACROSS = 4
PIECES = 8
WIDE = 256


def fused_kernel(
    queries_hbm, cond_hbm, shard_ref, row_ref, db_ref, gain_hbm, w_in_hbm, w_out_hbm, w_kv_ref,
    out_ref,
    wbuf, dbp, cond_ref, gain_ref, condf, xs, xv, keys, values, enc, part_send, part_recv, own_sum, y_send, y_recv,
    q_ref, w_in_ref, w_out_ref,
    local_sem, db_send, db_recv, w_send, w_recv, xs_send, xs_recv, sum_send, sum_recv,
):
    s = lax.axis_index("seq")
    t = lax.axis_index("tp")
    z, x = s // 2, s % 2
    core = t % 2
    flip = s + 1 - 2 * x
    sib = t + 1 - 2 * core
    ypeer = (t + 2) % 4
    stored = db_ref.shape[0]
    depth = w_kv_ref.shape[1]
    rows = enc.shape[0]
    e = enc.shape[1]
    off = pl.multiple_of(jnp.minimum(t * WIDE, e - WIDE), 128)

    barrier = pltpu.get_barrier_semaphore()
    for i in range(1, 8):
        pl.semaphore_signal(barrier, inc=1, device_id=((s + i) % 8, t), device_id_type=MESH)
    pl.semaphore_signal(barrier, inc=1, device_id=(s, sib), device_id_type=MESH)
    pl.semaphore_signal(barrier, inc=1, device_id=(s, ypeer), device_id_type=MESH)
    loads = [
        pltpu.make_async_copy(w_in_hbm, w_in_ref, local_sem.at[0]),
        pltpu.make_async_copy(w_out_hbm, w_out_ref, local_sem.at[1]),
        pltpu.make_async_copy(queries_hbm, q_ref, local_sem.at[2]),
        pltpu.make_async_copy(gain_hbm, gain_ref, local_sem.at[3]),
        pltpu.make_async_copy(cond_hbm.at[:, pl.ds(off, WIDE)], cond_ref, local_sem.at[4]),
        pltpu.make_async_copy(
            db_ref.at[:, :, pl.ds(off, WIDE)], dbp.at[pl.ds(s * stored, stored)], local_sem.at[5]
        ),
    ]
    for load in loads:
        load.start()
    pl.semaphore_wait(barrier, 9)

    def db_slot(b):
        return dbp.at[pl.ds(b * stored, stored)]

    def db_copy(src, b, way):
        target = (flip, s + 2, s - 2)[way]
        return pltpu.make_async_remote_copy(
            src_ref=src,
            dst_ref=db_slot(b),
            send_sem=db_send.at[way, b],
            recv_sem=db_recv.at[b],
            device_id=(target, t),
            device_id_type=MESH,
        )

    def db_arrival(b):
        return pltpu.make_async_copy(db_slot(b), db_slot(b), db_recv.at[b])

    def db_own(finish):
        own = db_ref.at[:, :, pl.ds(off, WIDE)]

        def do(copy):
            if finish:
                copy.wait_send()
            else:
                copy.start()

        @pl.when(z < ACROSS - 1)
        def _():
            do(db_copy(own, s, 1))

        @pl.when(z > 0)
        def _():
            do(db_copy(own, s, 2))

        do(db_copy(own, s, 0))

    def db_pass(hop, finish):
        for reached, b, further, way in (
            (z >= hop, s - 2 * hop, z < ACROSS - 1, 1),
            (z + hop < ACROSS, s + 2 * hop, z > 0, 2),
        ):
            @pl.when(reached)
            def _():
                if not finish:
                    db_arrival(b).wait()

                @pl.when(further)
                def _():
                    copy = db_copy(db_slot(b), b, way)
                    if finish:
                        copy.wait_send()
                    else:
                        copy.start()

                copy = db_copy(db_slot(b), b, 0)
                if finish:
                    copy.wait_send()
                else:
                    copy.start()

    db_own(False)

    def slot(p, b):
        return wbuf.at[p, pl.ds(pl.multiple_of(b * depth, 16), depth), :]

    def own_piece(p):
        return w_kv_ref.at[p % 2, :, pl.ds(pl.multiple_of((p // 2) * WIDE, WIDE), WIDE)]

    def w_copy(src, p, b, way):
        target = (flip, s + 2, s - 2)[way]
        return pltpu.make_async_remote_copy(
            src_ref=src,
            dst_ref=slot(p, b),
            send_sem=w_send.at[way, p, b],
            recv_sem=w_recv.at[p, b],
            device_id=(target, t),
            device_id_type=MESH,
        )

    def w_arrival(p, b):
        return pltpu.make_async_copy(slot(p, b), slot(p, b), w_recv.at[p, b])

    def own_start(p, carry):
        w_copy(own_piece(p), p, s, 0).start()

        @pl.when(z < ACROSS - 1)
        def _():
            w_copy(own_piece(p), p, s, 1).start()

        @pl.when(z > 0)
        def _():
            w_copy(own_piece(p), p, s, 2).start()

        pltpu.make_async_copy(own_piece(p), slot(p, s), w_recv.at[p, s]).start()
        return carry

    lax.fori_loop(0, 1, own_start, 0)

    def x_first(hop, finish):
        moves = [(z >= hop, -2 * hop, (1,)), (z + hop < ACROSS, 2 * hop, (2,))] if hop else [(z >= 0, 0, (1, 2))]
        for reached, shift, ways in moves:
            @pl.when(reached)
            def _():
                for base in (s, flip) if hop else (flip,):
                    b = base + shift
                    if not finish:
                        w_arrival(0, b).wait()
                    for way in ways:
                        @pl.when(z < ACROSS - 1 if way == 1 else z > 0)
                        def _():
                            copy = w_copy(slot(0, b), 0, b, way)
                            if finish:
                                copy.wait_send()
                            else:
                                copy.start()

    def pass_on(hop, first, last):
        def one(p, carry):
            @pl.when(z >= hop)
            def _():
                b = s - 2 * hop
                w_arrival(p, b).wait()
                w_copy(slot(p, b), p, b, 0).start()

                @pl.when(z < ACROSS - 1)
                def _():
                    w_copy(slot(p, b), p, b, 1).start()

            @pl.when(z + hop < ACROSS)
            def _():
                b = s + 2 * hop
                w_arrival(p, b).wait()
                w_copy(slot(p, b), p, b, 0).start()

                @pl.when(z > 0)
                def _():
                    w_copy(slot(p, b), p, b, 2).start()

            return carry

        lax.fori_loop(first, last, one, 0)

    for load in loads[3:]:
        load.wait()
    condf[...] = cond_ref[...].astype(jnp.float32)
    for hop in range(1, ACROSS):
        db_pass(hop, False)
    lax.fori_loop(1, PIECES, own_start, 0)
    for i in range(ACROSS):
        db_arrival(2 * i + 1 - x).wait()

    blocks = rows // 128

    def at_row(i):
        return pl.ds(i * 128, 128)

    def xs_copy(quarter, r, target, number):
        return pltpu.make_async_remote_copy(
            src_ref=xs.at[quarter, at_row(r)],
            dst_ref=xs.at[quarter, at_row(r)],
            send_sem=xs_send.at[number, r],
            recv_sem=xs_recv.at[quarter, r],
            device_id=(s, target),
            device_id_type=MESH,
        )

    def xs_arrival(quarter, r):
        here = xs.at[quarter, at_row(r)]
        return pltpu.make_async_copy(here, here, xs_recv.at[quarter, r])

    def pick(g, carry):
        for k in range(K):
            at = shard_ref[k, g] * stored + row_ref[k, g]
            picked = dbp[at].astype(jnp.float32) + condf[pl.ds(g, 1), :]
            xs[t, pl.ds(pl.multiple_of((g * K + k) * NL, NL), NL), :] = picked.astype(jnp.bfloat16)
        return carry

    per_block = 128 // (K * NL)
    for r in range(blocks):
        lax.fori_loop(r * per_block, (r + 1) * per_block, pick, 0)
        xs_copy(t, r, ypeer, 0).start()
        xs_copy(t, r, sib, 1).start()
    x_first(0, False)

    gain = gain_ref[...].astype(jnp.float32).reshape(1, e)
    theirs = (1 - core) * 64
    mine = core * 64

    def rows_of(r, inner):
        return pl.ds(pl.multiple_of(r * 128 + inner, 64), 64)

    def sum_copy(src, dst, target, number, r):
        return pltpu.make_async_remote_copy(
            src_ref=src,
            dst_ref=dst,
            send_sem=sum_send.at[number, r],
            recv_sem=sum_recv.at[number, r],
            device_id=(s, target),
            device_id_type=MESH,
        )

    def to_sib(r):
        return sum_copy(part_send.at[r], part_recv.at[r], sib, 0, r)

    def to_y(r):
        return sum_copy(y_send.at[r], y_recv.at[r], ypeer, 1, r)

    def to_share(r):
        return sum_copy(enc.at[rows_of(r, mine)], enc.at[rows_of(r, mine)], sib, 2, r)

    def share_arrival(r):
        here = enc.at[rows_of(r, theirs)]
        return pltpu.make_async_copy(here, here, sum_recv.at[2, r])

    def relay(r):
        xs_arrival(ypeer, r).wait()
        xs_copy(ypeer, r, sib, 2).start()

    def feed_forward(r):
        xs_arrival(sib, r).wait()
        xs_arrival((sib + 2) % 4, r).wait()
        at = at_row(r)
        whole = jnp.concatenate(
            [xs[0, at, :], xs[1, at, :], xs[2, at, :], xs[3, at, pl.ds(4 * WIDE - e, e - 3 * WIDE)]], axis=1
        )
        xv[at, :] = whole
        wide = whole.astype(jnp.float32)
        mean_square = jnp.mean(wide * wide, axis=1, keepdims=True)
        normed = (wide * lax.rsqrt(mean_square + 1e-06) * gain).astype(jnp.bfloat16)
        pre_act = lax.dot_general(
            normed, w_in_ref[...], (((1,), (1,)), ((), ())), preferred_element_type=jnp.float32
        )
        hidden = jax.nn.gelu(pre_act).astype(jnp.bfloat16)
        own_sum[at, :] = jnp.dot(hidden, w_out_ref[...], preferred_element_type=jnp.float32)
        part_send[r] = own_sum[rows_of(r, theirs), :].astype(jnp.bfloat16)
        to_sib(r).start()

    def add_sib(r):
        to_sib(r).wait_recv()
        own = own_sum[rows_of(r, mine), :] + part_recv[r].astype(jnp.float32)
        own_sum[rows_of(r, mine), :] = own
        y_send[r] = own.astype(jnp.bfloat16)
        to_y(r).start()

    def share(r):
        to_y(r).wait_recv()
        where = rows_of(r, mine)
        total = own_sum[where, :] + y_recv[r].astype(jnp.float32)
        enc[where, :] = (xv[where, :].astype(jnp.float32) + total).astype(jnp.bfloat16)
        to_share(r).start()

    loads[0].wait()
    loads[1].wait()
    relay(0)
    x_first(1, False)
    for r in range(blocks):
        if r + 1 < blocks:
            relay(r + 1)
        feed_forward(r)
        if r:
            add_sib(r - 1)
        pass_on(1, 1 + 2 * r, min(3 + 2 * r, PIECES))
    add_sib(blocks - 1)
    x_first(2, False)
    for r in range(blocks):
        pass_on(2, 1 + 2 * r, min(3 + 2 * r, PIECES))
        share(r)
    x_first(3, False)
    pass_on(3, 1, 4)
    for r in range(blocks):
        share_arrival(r).wait()
    loads[2].wait()

    span = 4 * K * NL
    qspan = 4 * GROUP
    tall = lax.broadcasted_iota(jnp.int32, (qspan, span), 0) // GROUP
    flat = lax.broadcasted_iota(jnp.int32, (qspan, span), 1) // (K * NL)
    inside = tall == flat
    scale = HEAD ** -0.5 * 1.4426950408889634
    ones = jnp.ones((span, HEAD), jnp.bfloat16)

    def chunk(c, carry):
        for j in range(2):
            p = 2 * c + j
            pltpu.make_async_copy(own_piece(p), slot(p, s), w_recv.at[p, s]).wait()

            @pl.when(p > 0)
            def _():
                for i in range(ACROSS):
                    w_arrival(p, 2 * i + 1 - x).wait()

        pass_on(3, jnp.minimum(2 * c + 4, PIECES), jnp.minimum(2 * c + 6, PIECES))
        block = enc[...]
        keys[...] = jnp.dot(block, wbuf[2 * c], preferred_element_type=jnp.float32).astype(jnp.bfloat16)
        values[...] = jnp.dot(block, wbuf[2 * c + 1], preferred_element_type=jnp.float32).astype(jnp.bfloat16)
        for h in range(WIDE // HEAD):
            cols = pl.ds(pl.multiple_of(c * WIDE + h * HEAD, HEAD), HEAD)
            part = slice(h * HEAD, (h + 1) * HEAD)
            for i in range(rows // span):
                krows = slice(i * span, (i + 1) * span)
                qrows = slice(i * qspan, (i + 1) * qspan)
                scores = lax.dot_general(
                    q_ref[qrows, cols], keys[krows, part], (((1,), (1,)), ((), ())),
                    preferred_element_type=jnp.float32,
                )
                scores = jnp.where(inside, scores * scale, -jnp.inf)
                top = jnp.max(scores, axis=1, keepdims=True)
                grown = jnp.exp2(scores - top).astype(jnp.bfloat16)
                both = jnp.concatenate([values[krows, part], ones], axis=1)
                mixed = jnp.dot(grown, both, preferred_element_type=jnp.float32)
                out_ref[qrows, cols] = (mixed[:, :HEAD] / mixed[:, HEAD:]).astype(jnp.bfloat16)
        return carry

    lax.fori_loop(0, PIECES // 2, chunk, 0)

    db_own(True)
    for hop in range(1, ACROSS):
        db_pass(hop, True)
    for r in range(blocks):
        xs_copy(t, r, ypeer, 0).wait_send()
        xs_copy(t, r, sib, 1).wait_send()
        xs_copy(ypeer, r, sib, 2).wait_send()
        to_sib(r).wait_send()
        to_y(r).wait_send()
        to_share(r).wait_send()

    for hop in range(ACROSS):
        x_first(hop, True)

    def sends_done(p, carry):
        w_copy(own_piece(p), p, s, 0).wait_send()

        @pl.when(z < ACROSS - 1)
        def _():
            w_copy(own_piece(p), p, s, 1).wait_send()

        @pl.when(z > 0)
        def _():
            w_copy(own_piece(p), p, s, 2).wait_send()

        @pl.when(p > 0)
        def _():
            for hop in range(1, ACROSS):
                @pl.when(z >= hop)
                def _():
                    b = s - 2 * hop
                    w_copy(slot(p, b), p, b, 0).wait_send()

                    @pl.when(z < ACROSS - 1)
                    def _():
                        w_copy(slot(p, b), p, b, 1).wait_send()

                @pl.when(z + hop < ACROSS)
                def _():
                    b = s + 2 * hop
                    w_copy(slot(p, b), p, b, 0).wait_send()

                    @pl.when(z > 0)
                    def _():
                        w_copy(slot(p, b), p, b, 2).wait_send()

        return carry

    lax.fori_loop(0, PIECES, sends_done, 0)


def fused_body(queries, group_cond, nbr_shard, nbr_row, database, enc_gain, w_in, w_out, w_kv):
    bf16, f32 = jnp.bfloat16, jnp.float32
    rows = nbr_shard.shape[0] * K * NL
    blocks = rows // 128
    vmem = pl.BlockSpec(memory_space=pltpu.VMEM)
    smem = pl.BlockSpec(memory_space=pltpu.SMEM)
    hbm = pl.BlockSpec(memory_space=pltpu.HBM)
    dma = pltpu.SemaphoreType.DMA
    return pl.pallas_call(
        fused_kernel,
        out_shape=jax.ShapeDtypeStruct(queries.shape, bf16),
        in_specs=[hbm, hbm, smem, smem, hbm, hbm, hbm, hbm, hbm],
        out_specs=vmem,
        scratch_shapes=[
            pltpu.VMEM((PIECES, E, WIDE), bf16),
            pltpu.VMEM((8 * database.shape[0], NL, WIDE), bf16),
            pltpu.VMEM((group_cond.shape[0], WIDE), bf16),
            pltpu.VMEM(enc_gain.shape, bf16),
            pltpu.VMEM((group_cond.shape[0], WIDE), f32),
            pltpu.VMEM((4, rows, WIDE), bf16),
            pltpu.VMEM((rows, E), bf16),
            pltpu.VMEM((rows, WIDE), bf16),
            pltpu.VMEM((rows, WIDE), bf16),
            pltpu.VMEM((rows, E), bf16),
            pltpu.VMEM((blocks, 64, E), bf16),
            pltpu.VMEM((blocks, 64, E), bf16),
            pltpu.VMEM((rows, E), f32),
            pltpu.VMEM((blocks, 64, E), bf16),
            pltpu.VMEM((blocks, 64, E), bf16),
            pltpu.VMEM(queries.shape, bf16),
            pltpu.VMEM(w_in.shape, bf16),
            pltpu.VMEM(w_out.shape, bf16),
            dma((6,)),
            dma((3, 8)),
            dma((8,)),
            dma((3, PIECES, 8)),
            dma((PIECES, 8)),
            dma((3, blocks)),
            dma((4, blocks)),
            dma((3, blocks)),
            dma((3, blocks)),
        ],
        compiler_params=pltpu.CompilerParams(
            collective_id=0, has_side_effects=True, vmem_limit_bytes=62 * 1024 * 1024
        ),
    )(queries, group_cond, nbr_shard.T, nbr_row.T, database, enc_gain, w_in, w_out, w_kv)


def solution(mesh):
    placed = (
        P("seq", "tp"),
        P("seq", None),
        P("seq", None),
        P("seq", None),
        P("seq", None, None),
        P(),
        P("tp", None),
        P("tp", None),
        P(None, "seq", "tp"),
    )
    fused = mesh.shape["seq"] == 8 and mesh.shape["tp"] == 4
    return jax.shard_map(
        fused_body if fused else body, mesh=mesh, in_specs=placed, out_specs=P("seq", "tp"), check_vma=False
    )
```
